512 devices in a mesh: dom: 128 (over z, y, core), hub: 4 (over x).
Axes of the slice: x: 4, y: 8, z: 8, core: 2. Of those that a mesh axis runs over, the one named last changes fastest.
Arguments:
- user_cot: float32 [16384, 256], P('dom'), may hold values from -6 to 6
- hub_adj: float32 [16384, 2048], P('dom', 'hub'), may hold values from -0.09375 to 0.09375
- tiles: float32 [65536, 8, 128], P(('dom', 'hub')), may hold values from -0.125 to 0.125
- tile_index: int32 [3, 65536], P(None, ('dom', 'hub')), may hold values from 0 to 127, as said below
- hub_mask: int32 [2, 2048, 256], P(None, 'hub'), may hold values 0 or 1
- tail_mask: int32 [2, 32768, 256], P(None, 'dom'), may hold values 0 or 1
Outputs:
- user_grad: float32 [16384, 256], P('dom')
- hub_grad: float32 [2048, 256], P('hub')
- tail_grad: float32 [32768, 256], P('dom')
The draws below stay inside these ranges and needn't reach their ends.
Inputs may be any that keep to these rules, and one draw needn't show every extreme that they name: `tile_index`: row 0 is a tile's user block within its own partition (below 1), row 1 the partition that owns its items (below 128 partitions, i.e. 16384 / 128), row 2 the item block within that partition (below 32). Rows 1 and 2 are the same, position by position, on all 4 hub shards of one partition. No device holds more than 2 tiles whose items one partition owns. One particular partition receives exactly 2 tiles from every device; any other partition receives 0, 1 or 2 tiles from a device.
All inputs are finite; a program needn't handle non-finite values. No bound on the sum of `hub_mask` or of `tail_mask` on one device may be relied on, other than what follows from the above.
Results may differ from the reference program's by a relative error of at most 0.0001.
Values sent between devices are 32-bit elements; how exact they have to be, the bound alone decides.
A program may use at most 64 MiB of HBM per device.

```python
import jax
import jax.numpy as jnp
from jax import lax

F = 256
HUB = 2048
UBLK = 128
IB = 8
TRIPS = 2
USR_DEV = 128
TAIL_DEV = 256
NT = 128
USERS = 16384
TAIL = 32768
NT_ALL = 65536
CAP = 2
N_DOM = 128
N_HUB = 4


def draw_tile_index(key, part):
    common = jax.random.randint(jax.random.fold_in(key, 11), (), 0, N_DOM).astype(jnp.int32)

    def device_draw(device_flat):
        group_key = jax.random.fold_in(jax.random.fold_in(key, 29), device_flat // N_HUB)
        own_key = jax.random.fold_in(jax.random.fold_in(key, 31), device_flat)
        key_one, key_two, key_three, key_five = jax.random.split(group_key, 4)
        others = jax.random.permutation(key_one, N_DOM - 1).astype(jnp.int32)
        others = others + (others >= common).astype(jnp.int32)
        pool_peers = others[jnp.arange((N_DOM - 1) * CAP, dtype=jnp.int32) // CAP]
        pool_peers = jax.random.permutation(key_two, pool_peers)
        owners = jnp.concatenate([jnp.full((CAP,), common, jnp.int32), pool_peers[:NT - CAP]])
        owners = jax.random.permutation(key_three, owners)
        user_block = jax.random.randint(own_key, (NT,), 0, USR_DEV // UBLK).astype(jnp.int32)
        item_block = jax.random.randint(key_five, (NT,), 0, TAIL_DEV // IB).astype(jnp.int32)
        return jnp.stack([user_block, owners, item_block])
    columns = jax.vmap(device_draw)(jnp.arange(N_DOM * N_HUB, dtype=jnp.int32))
    return jnp.transpose(columns, (1, 0, 2)).reshape(3, N_DOM * N_HUB * NT)


def place_ends(array, rng, low, high):
    place = [jax.random.randint(jax.random.fold_in(rng, axis), (), 0, length) for axis, length in enumerate(array.shape)]
    longest = array.shape.index(max(array.shape))
    next_to = place[:longest] + [(place[longest] + 1) % array.shape[longest]] + place[longest + 1:]
    return array.at[tuple(place)].set(low).at[tuple(next_to)].set(high)


def levels(key, extent, pieces, smallest, high):
    def one(position, blocks):
        steps = jax.random.uniform(jax.random.fold_in(jax.random.fold_in(key, 6), position), (blocks,), jnp.float32, smallest / len(pieces), high / len(pieces))
        return jnp.repeat(jnp.exp(steps), extent[position] // blocks).reshape((-1,) + (1,) * (len(extent) - position - 1))

    loudness = one(*pieces[0])
    for cut in pieces[1:]:
        loudness = loudness * one(*cut)
    return loudness


def gaussian(key, shape, width, bound, pieces=(), kind=jnp.bfloat16):
    factor_of = levels(key, shape, pieces, -0.22, 0.18) if pieces else 1.0
    drawn = jax.random.normal(key, shape, jnp.float32) * width * factor_of
    return jnp.minimum(jnp.maximum(drawn, -bound), bound).astype(kind)


def setup_inputs(seed: int = 0) -> dict:
    arg_keys = jax.random.split(jax.random.key(seed), 7)
    user_cot = gaussian(arg_keys[0], (USERS, F), 1.0, 6.0, ((0, 128),), jnp.float32)
    hub_adj = gaussian(arg_keys[1], (USERS, HUB), ((USERS * HUB // 2) ** 0.5) ** -0.5, 0.09375, ((0, 128), (1, 4)), jnp.float32)
    tiles = gaussian(arg_keys[2], (NT_ALL, IB, UBLK), (NT * N_HUB * UBLK * IB // TAIL_DEV) ** -0.5, 0.125, ((0, 512),), jnp.float32)
    tile_index = draw_tile_index(jax.random.fold_in(arg_keys[6], 71), 0)
    hub_mask = place_ends((jax.random.randint(arg_keys[4], (TRIPS, HUB, F), 0, 4) < 3).astype(jnp.int32), jax.random.fold_in(arg_keys[4], 1), 0, 1)
    tail_mask = place_ends((jax.random.randint(arg_keys[5], (TRIPS, TAIL, F), 0, 4) < 3).astype(jnp.int32), jax.random.fold_in(arg_keys[5], 1), 0, 1)
    return dict(user_cot=user_cot, hub_adj=hub_adj, tiles=tiles, tile_index=tile_index, hub_mask=hub_mask, tail_mask=tail_mask)


def reference(user_cot, hub_adj, tiles, tile_index, hub_mask, tail_mask):
    precise = lax.Precision.HIGHEST
    tile_total = tiles.shape[0]
    holder = jnp.arange(tile_total, dtype=jnp.int32) // (NT * N_HUB)
    user_first = holder * USR_DEV + tile_index[0] * UBLK
    item_first = tile_index[1] * TAIL_DEV + tile_index[2] * IB
    user_lists = (user_first[:, None] + jnp.arange(UBLK, dtype=jnp.int32)[None, :]).reshape(-1, NT, UBLK)
    item_lists = (item_first[:, None] + jnp.arange(IB, dtype=jnp.int32)[None, :]).reshape(-1, NT, IB)
    tile_groups = tiles.reshape(-1, NT, IB, UBLK)
    gradient = user_cot
    hub_grad = None
    tail_grad = None
    for trip_index in range(TRIPS):
        hub_grad = jnp.dot(hub_adj.T, gradient, precision=precise, preferred_element_type=jnp.float32)
        hub_grad = hub_grad * hub_mask[trip_index].astype(jnp.float32)

        def to_items(running, group):
            tile_block, user_rows, item_rows = group
            contrib = jnp.einsum("kiu,kuf->kif", tile_block, gradient[user_rows], precision=precise)
            return running.at[item_rows.reshape(-1)].add(contrib.reshape(-1, F)), None

        tail_grad, _ = lax.scan(to_items, jnp.zeros((TAIL, F), jnp.float32), (tile_groups, user_lists, item_lists))
        tail_grad = tail_grad * tail_mask[trip_index].astype(jnp.float32)
        tail_now = tail_grad

        def to_users(running, group):
            tile_block, user_rows, item_rows = group
            contrib = jnp.einsum("kiu,kif->kuf", tile_block, tail_now[item_rows], precision=precise)
            return running.at[user_rows.reshape(-1)].add(contrib.reshape(-1, F)), None

        start_users = jnp.dot(hub_adj, hub_grad, precision=precise, preferred_element_type=jnp.float32)
        gradient, _ = lax.scan(to_users, start_users, (tile_groups, user_lists, item_lists))
    return gradient, hub_grad, tail_grad
```

```python
import jax
import jax.numpy as jnp
from jax import lax
from jax.experimental import pallas as pl
from jax.experimental.pallas import tpu as pltpu
from jax.sharding import PartitionSpec as P

F32 = jnp.float32
BF16 = jnp.bfloat16
MESH = pl.DeviceIdType.MESH

(PAIR_RS, ONE_RS, TWO_RS, TWO_AG, ONE_AG, PAIR_AG, TAIL_F, TAIL_R, HUB_RS, HUB_AG, TAIL_OUT, TILE_RS, TILE_AG, INDEX) = range(14)
KINDS = 14


def split(x):
    hi = x.astype(BF16)
    return hi, (x - hi.astype(F32)).astype(BF16)


def dot(a, b, dims=((1,), (0,))):
    return lax.dot_general(a, b, (dims, ((), ())), preferred_element_type=F32)


def dot3(ah, al, bh, bl):
    return dot(ah, bh) + dot(ah, bl) + dot(al, bh)


def lanes(shape):
    return lax.broadcasted_iota(jnp.int32, shape, len(shape) - 1)


def rows(shape):
    return lax.broadcasted_iota(jnp.int32, shape, len(shape) - 2)


def roll64(x):
    return pltpu.roll(x, 64, 1)


def side_by_side(hi, lo):
    return jnp.concatenate([hi, lo], axis=1)


def fold(x):
    return x[:, :128] + x[:, 128:]


def kernel(
    cot_ref, hub_adj_ref, tiles_ref, index_ref, hub_mask_ref, tail_mask_ref,
    user_out, hub_out, tail_out,
    tile_in, tile_sum, slot_index, index_in, tile_hi, tile_lo, tile_t_hi, tile_t_lo, member, member_t,
    hubp, pair_in, one_out, one_in, two_out, two_in, hub_full,
    tail_send, tail_recv, reply_send, reply_recv, user_pack, user_in, grad_pack, tail_pack, grad_ref,
    send_sem, recv_sem,
):
    d = lax.axis_index("dom")
    j = lax.axis_index("hub")
    core = lax.rem(d, 2)
    y = lax.rem(d // 2, 8)
    z = d // 16
    a1 = y * (1 - core) + z * core
    a2 = z * (1 - core) + y * core
    stride1 = 2 * (1 - core) + 16 * core
    stride2 = 16 * (1 - core) + 2 * core
    base1 = d - a1 * stride1
    base2 = d - a2 * stride2
    partner = d + 1 - 2 * core

    def send(src, dst, t, kind, dom, hub):
        pltpu.make_async_remote_copy(
            src_ref=src, dst_ref=dst, send_sem=send_sem.at[t, kind], recv_sem=recv_sem.at[t, kind],
            device_id=(dom, hub), device_id_type=MESH,
        ).start()

    def wait_in(ref, t, kind):
        pltpu.make_async_copy(ref, ref, recv_sem.at[t, kind]).wait()

    def wait_out(ref, t, kind):
        pltpu.make_async_copy(ref, ref, send_sem.at[t, kind]).wait()

    def peers_all(body):
        def step(k, carry):
            body(lax.rem(d + k, 128))
            body(lax.rem(d + 128 - k, 128))
            return carry
        lax.fori_loop(1, 64, step, 0)
        body(lax.rem(d + 64, 128))

    def peers_hub(body):
        for o in (1, 3, 2):
            body(lax.rem(j + o, 4), o - 1)

    barrier = pltpu.get_barrier_semaphore()
    peers_all(lambda p: pl.semaphore_signal(barrier, inc=1, device_id=(p, j), device_id_type=MESH))
    peers_hub(lambda h, o: pl.semaphore_signal(barrier, inc=1, device_id=(d, h), device_id_type=MESH))
    pl.semaphore_wait(barrier, 130)

    peers_hub(lambda h, o: send(tiles_ref.at[pl.ds(h * 32, 32)], tile_in.at[o], 0, TILE_RS, d, h))

    owner_row = jnp.broadcast_to(index_ref[1:2, :], (128, 128))
    block_row = jnp.broadcast_to(index_ref[2:3, :], (128, 128)).astype(F32)
    square = (128, 128)
    earlier = (owner_row == owner_row.astype(F32).T.astype(jnp.int32)) & (rows(square) < lanes(square))
    rank = jnp.sum(earlier.astype(F32), axis=0, keepdims=True)
    owned = owner_row == rows(square)
    pick0 = (owned & (rank < 0.5)).astype(F32)
    pick1 = (owned & (rank > 0.5)).astype(F32)
    block0 = jnp.sum(pick0 * block_row, axis=1, keepdims=True)
    block1 = jnp.sum(pick1 * block_row, axis=1, keepdims=True)
    slot_index[...] = jnp.where(lanes(square) < 64, block0, block1).reshape(128, 1, 128)
    index_in[pl.ds(d, 1)] = slot_index[pl.ds(d, 1)]
    peers_all(lambda p: send(slot_index.at[p], index_in.at[d], 0, INDEX, p, j))

    adj = hub_adj_ref[...]
    adj_hi, adj_lo = split(adj)
    adj_t_hi, adj_t_lo = split(adj.T)

    def hub_start(t, grad):
        gh, gl = split(grad)
        hubp[t] = dot3(adj_t_hi, adj_t_lo, gh, gl)
        send(hubp.at[t, pl.ds((1 - core) * 256, 256)], pair_in.at[t], t, PAIR_RS, partner, j)

    def hub_one(t):
        wait_in(pair_in.at[t], t, PAIR_RS)
        one_out[t] = (hubp[t, pl.ds(core * 256, 256)] + pair_in[t]).reshape(8, 32, 256)
        for o in (1, 7, 2, 6, 3, 5, 4):
            g = lax.rem(a1 + o, 8)
            send(one_out.at[t, g], one_in.at[t, o - 1], t, ONE_RS, base1 + g * stride1, j)

    def hub_two(t):
        wait_in(one_in.at[t], t, ONE_RS)
        total = one_out[t, a1]
        for o in range(7):
            total = total + one_in[t, o]
        for b in range(4):
            for h in range(2):
                two_out[t, 2 * b + h] = total[8 * b:8 * b + 8, 128 * h:128 * h + 128]
        for o in (1, 7, 2, 6, 3, 5, 4):
            g = lax.rem(a2 + o, 8)
            send(two_out.at[t, g], two_in.at[t, o - 1], t, TWO_RS, base2 + g * stride2, j)

    def hub_back_two(t):
        wait_in(two_in.at[t], t, TWO_RS)
        total = two_out[t, a2]
        for o in range(7):
            total = total + two_in[t, o]
        first = pl.multiple_of(core * 256 + a1 * 32 + (a2 // 2) * 8, 8)
        left = pl.multiple_of(lax.rem(a2, 2) * 128, 128)
        mask = hub_mask_ref[t, pl.ds(first, 8), pl.ds(left, 128)].astype(F32)
        hub_full[t, core, a1, a2] = total * mask
        for o in (1, 7, 2, 6, 3, 5, 4):
            g = lax.rem(a2 + o, 8)
            send(hub_full.at[t, core, a1, a2], hub_full.at[t, core, a1, a2], t, TWO_AG, base2 + g * stride2, j)

    def hub_back_one(t):
        wait_in(two_in.at[t], t, TWO_AG)
        for o in (1, 7, 2, 6, 3, 5, 4):
            g = lax.rem(a1 + o, 8)
            send(hub_full.at[t, core, a1], hub_full.at[t, core, a1], t, ONE_AG, base1 + g * stride1, j)

    def hub_back_pair(t):
        wait_in(one_in.at[t], t, ONE_AG)
        send(hub_full.at[t, core], hub_full.at[t, core], t, PAIR_AG, partner, j)

    def hub_finish(t):
        wait_in(pair_in.at[t], t, PAIR_AG)
        full = hub_full[t].reshape(64, 2, 8, 128)
        item = jnp.concatenate([full[:, 0].reshape(512, 128), full[:, 1].reshape(512, 128)], axis=1)
        if t == 1:
            hub_out[...] = item
        ih, il = split(item)
        part = dot3(adj_hi, adj_lo, ih, il)
        low = lanes((64, 128)) < 64
        for h in range(4):
            half = part[:, 128 * (h // 2):128 * (h // 2) + 128]
            if h % 2 == 0:
                user_pack[t, h] = jnp.where(low, half[:64], roll64(half[64:]))
            else:
                user_pack[t, h] = jnp.where(low, roll64(half[:64]), half[64:])
        peers_hub(lambda h, o: send(user_pack.at[t, h], user_in.at[t, o], t, HUB_RS, d, h))

    left_half = pl.multiple_of((j // 2) * 128, 128)
    odd = lax.rem(j, 2)

    def mine(half):
        kept = jnp.where((lanes(half.shape) // 64) == odd, half, 0.0)
        return kept + roll64(kept)

    def halves(x):
        low = lanes(x.shape) < 64
        return jnp.concatenate([jnp.where(low, x, 0.0), jnp.where(low, 0.0, x)], axis=0)

    def tail_start(t, half):
        bh, bl = split(halves(mine(half)))
        both = side_by_side(bh, bl)
        for q in range(4):
            part = slice(256 * q, 256 * q + 256)
            x = fold(dot(tile_hi[part], both)) + dot(tile_lo[part], bh)
            tail_send[t, 32 * q:32 * q + 32] = x.reshape(32, 8, 128)
        tail_recv[t, d] = tail_send[t, d]
        peers_all(lambda p: send(tail_send.at[t, p], tail_recv.at[t, d], t, TAIL_F, p, j))

    def tail_turn(t):
        wait_in(tail_recv.at[t, pl.ds(0, 127)], t, TAIL_F)
        hi, lo = split(tail_recv[t].reshape(1024, 128))
        x = fold(dot(member[...], side_by_side(hi, lo)))
        low = lanes((256, 128)) < 64
        item = jnp.where(low, x[:256], x[256:])
        item = item + roll64(item)
        item = item * mine(tail_mask_ref[t, :, pl.ds(left_half, 128)].astype(F32))
        ih, il = split(halves(item))
        both = side_by_side(ih, il)
        for q in range(4):
            x = fold(dot(member_t[256 * q:256 * q + 256], both))
            reply_send[t, 32 * q:32 * q + 32] = x.reshape(32, 8, 128)
        reply_recv[t, d] = reply_send[t, d]
        peers_all(lambda p: send(reply_send.at[t, p], reply_recv.at[t, d], t, TAIL_R, p, j))
        if t == 1:
            tail_pack[j] = jnp.where(lanes((128, 128)) < 64, item[:128], item[128:])
            peers_hub(lambda h, o: send(tail_pack.at[j], tail_pack.at[j], 0, TAIL_OUT, d, h))

    def tail_end(t):
        wait_in(reply_recv.at[t, pl.ds(0, 127)], t, TAIL_R)
        rh, rl = split(reply_recv[t].reshape(1024, 128))
        x = fold(dot(tile_t_hi[...], side_by_side(rh, rl))) + dot(tile_t_lo[...], rh)
        low = lanes((64, 128)) < 64
        return jnp.where(low, x[:64] + roll64(x[128:192]), roll64(x[64:128]) + x[192:])

    def join(t, packed):
        wait_in(user_in.at[t], t, HUB_RS)
        grad_pack[t, j] = packed + user_pack[t, j] + user_in[t, 0] + user_in[t, 1] + user_in[t, 2]
        peers_hub(lambda h, o: send(grad_pack.at[t, j], grad_pack.at[t, j], t, HUB_AG, d, h))
        wait_in(user_in.at[t], t, HUB_AG)
        low = lanes((64, 128)) < 64
        out = user_out if t == 1 else grad_ref
        for k in range(2):
            even, uneven = grad_pack[t, 2 * k], grad_pack[t, 2 * k + 1]
            out[:64, 128 * k:128 * k + 128] = jnp.where(low, even, roll64(uneven))
            out[64:, 128 * k:128 * k + 128] = jnp.where(low, roll64(even), uneven)

    hub_start(0, cot_ref[...])
    wait_in(tile_in, 0, TILE_RS)
    own = pl.ds(j * 32, 32)
    tile_sum[own] = tiles_ref[own] + tile_in[0] + tile_in[1] + tile_in[2]
    peers_hub(lambda h, o: send(tile_sum.at[own], tile_sum.at[own], 0, TILE_AG, d, h))
    hub_one(0)
    wait_in(tile_in, 0, TILE_AG)

    th, tl = split(tile_sum[...].reshape(128, 1024))
    both = jnp.concatenate([th, tl], axis=1)
    for s, pick in ((0, pick0), (1, pick1)):
        x = dot(pick.astype(BF16), both)
        placed = (x[:, :1024] + x[:, 1024:]).reshape(1024, 128)
        hi, lo = split(placed)
        tile_hi[:, 128 * s:128 * s + 128] = hi
        tile_lo[:, 128 * s:128 * s + 128] = lo
        hi, lo = split(placed.T)
        tile_t_hi[128 * s:128 * s + 128] = hi
        tile_t_lo[128 * s:128 * s + 128] = lo
    tail_start(0, cot_ref[:, pl.ds(left_half, 128)])
    hub_two(0)

    wait_in(index_in.at[pl.ds(0, 127)], 0, INDEX)
    spread = (rows((1024, 128)) // 8 == lanes((1024, 128))).astype(BF16)
    blocks = dot(spread, index_in[...].reshape(128, 128).astype(BF16))
    place = blocks * 8.0 + lax.rem(rows((1024, 128)), 8).astype(F32)
    place_t = place.T
    want_t = lanes((1024, 256)).astype(F32)
    want = rows((256, 1024)).astype(F32)
    for s in range(2):
        member_t[:, 256 * s:256 * s + 256] = (place[:, 64 * s:64 * s + 1] == want_t).astype(F32).astype(BF16)
        member[256 * s:256 * s + 256] = (place_t[64 * s:64 * s + 1] == want).astype(F32).astype(BF16)

    for t in range(2):
        if t == 1:
            hub_start(1, grad_ref[...])
            tail_start(1, grad_ref[:, pl.ds(left_half, 128)])
            hub_one(1)
            hub_two(1)
        hub_back_two(t)
        hub_back_one(t)
        hub_back_pair(t)
        tail_turn(t)
        hub_finish(t)
        join(t, tail_end(t))

    wait_in(tail_pack.at[pl.ds(0, 3)], 0, TAIL_OUT)
    low = lanes((128, 128)) < 64
    for k in range(2):
        even, uneven = tail_pack[2 * k], tail_pack[2 * k + 1]
        tail_out[:128, 128 * k:128 * k + 128] = jnp.where(low, even, roll64(uneven))
        tail_out[128:, 128 * k:128 * k + 128] = jnp.where(low, roll64(even), uneven)

    wait_out(tile_in, 0, TILE_RS)
    wait_out(tile_in, 0, TILE_AG)
    wait_out(index_in.at[pl.ds(0, 127)], 0, INDEX)
    wait_out(tail_pack.at[pl.ds(0, 3)], 0, TAIL_OUT)
    for t in range(2):
        wait_out(pair_in.at[t], t, PAIR_RS)
        wait_out(one_in.at[t], t, ONE_RS)
        wait_out(two_in.at[t], t, TWO_RS)
        wait_out(two_in.at[t], t, TWO_AG)
        wait_out(one_in.at[t], t, ONE_AG)
        wait_out(pair_in.at[t], t, PAIR_AG)
        wait_out(tail_recv.at[t, pl.ds(0, 127)], t, TAIL_F)
        wait_out(reply_recv.at[t, pl.ds(0, 127)], t, TAIL_R)
        wait_out(user_in.at[t], t, HUB_RS)
        wait_out(user_in.at[t], t, HUB_AG)


def local(user_cot, hub_adj, tiles, tile_index, hub_mask, tail_mask):
    vmem = pl.BlockSpec(memory_space=pltpu.VMEM)
    return pl.pallas_call(
        kernel,
        out_shape=(
            jax.ShapeDtypeStruct((128, 256), F32),
            jax.ShapeDtypeStruct((512, 256), F32),
            jax.ShapeDtypeStruct((256, 256), F32),
        ),
        in_specs=[vmem] * 6,
        out_specs=(vmem,) * 3,
        scratch_shapes=[
            pltpu.VMEM((3, 32, 8, 128), F32),
            pltpu.VMEM((128, 8, 128), F32),
            pltpu.VMEM((128, 1, 128), F32),
            pltpu.VMEM((128, 1, 128), F32),
            pltpu.VMEM((1024, 256), BF16),
            pltpu.VMEM((1024, 256), BF16),
            pltpu.VMEM((256, 1024), BF16),
            pltpu.VMEM((256, 1024), BF16),
            pltpu.VMEM((512, 1024), BF16),
            pltpu.VMEM((1024, 512), BF16),
            pltpu.VMEM((2, 512, 256), F32),
            pltpu.VMEM((2, 256, 256), F32),
            pltpu.VMEM((2, 8, 32, 256), F32),
            pltpu.VMEM((2, 7, 32, 256), F32),
            pltpu.VMEM((2, 8, 8, 128), F32),
            pltpu.VMEM((2, 7, 8, 128), F32),
            pltpu.VMEM((2, 2, 8, 8, 8, 128), F32),
            pltpu.VMEM((2, 128, 8, 128), F32),
            pltpu.VMEM((2, 128, 8, 128), F32),
            pltpu.VMEM((2, 128, 8, 128), F32),
            pltpu.VMEM((2, 128, 8, 128), F32),
            pltpu.VMEM((2, 4, 64, 128), F32),
            pltpu.VMEM((2, 3, 64, 128), F32),
            pltpu.VMEM((2, 4, 64, 128), F32),
            pltpu.VMEM((4, 128, 128), F32),
            pltpu.VMEM((128, 256), F32),
            pltpu.SemaphoreType.DMA((2, KINDS)),
            pltpu.SemaphoreType.DMA((2, KINDS)),
        ],
        compiler_params=pltpu.CompilerParams(
            collective_id=0, has_side_effects=True, vmem_limit_bytes=48 * 1024 * 1024
        ),
        cost_estimate=pl.CostEstimate(flops=4_000_000_000, bytes_accessed=4_000_000, transcendentals=0),
    )(user_cot, hub_adj, tiles, tile_index, hub_mask, tail_mask)


def solution(mesh):
    return jax.shard_map(
        local,
        mesh=mesh,
        in_specs=(
            P("dom", None),
            P("dom", "hub"),
            P(("dom", "hub"), None, None),
            P(None, ("dom", "hub")),
            P(None, "hub", None),
            P(None, "dom", None),
        ),
        out_specs=(P("dom", None), P("hub", None), P("dom", None)),
        check_vma=False,
    )
```

```python
import jax
import jax.numpy as jnp
from jax import lax
from jax.experimental import pallas as pl
from jax.experimental.pallas import tpu as pltpu
from jax.sharding import PartitionSpec as P

F32 = jnp.float32
BF16 = jnp.bfloat16
MESH = pl.DeviceIdType.MESH

(PAIR_RS, ONE_RS, TWO_RS, TWO_AG, ONE_AG, PAIR_AG, TAIL_F, TAIL_R,
 HUB_RS, HUB_AG, TAIL_OUT, INDEX_ONE, INDEX_TWO, TILE_RS, TILE_AG) = range(15)
CUTS = 4
KINDS = 14 + 2 * CUTS
AROUND = (4, 1, 7, 3, 5, 2, 6)


def split(x):
    hi = x.astype(BF16)
    return hi, (x - hi.astype(F32)).astype(BF16)


def dot(a, b, dims=((1,), (0,))):
    return lax.dot_general(a, b, (dims, ((), ())), preferred_element_type=F32)


def dot3(ah, al, bh, bl):
    return dot(ah, bh) + dot(ah, bl) + dot(al, bh)


def lanes(shape):
    return lax.broadcasted_iota(jnp.int32, shape, len(shape) - 1)


def rows(shape):
    return lax.broadcasted_iota(jnp.int32, shape, len(shape) - 2)


def roll64(x):
    return pltpu.roll(x, 64, 1)


def side_by_side(hi, lo):
    return jnp.concatenate([hi, lo], axis=1)


def fold(x):
    return x[:, :128] + x[:, 128:]


def kernel(
    cot_hbm, hub_adj_hbm, tiles_hbm, index_hbm, hub_mask_hbm, tail_mask_hbm,
    user_out, hub_out, tail_out,
    cot_ref, hub_adj_ref, tiles_ref, index_ref, hub_mask_ref, tail_mask_ref, load_sem,
    tile_in, tile_sum, slot_index, index_mid, index_in, tile_hi, tile_lo, tile_t_hi, tile_t_lo, member, member_t,
    hubp, pair_in, one_out, one_in, two_out, two_in, hub_full,
    tail_send, tail_recv, reply_send, reply_recv, user_pack, user_in, grad_pack, tail_pack, grad_ref,
    send_sem, recv_sem,
):
    d = lax.axis_index("dom")
    j = lax.axis_index("hub")
    core = lax.rem(d, 2)
    y = lax.rem(d // 2, 8)
    z = d // 16
    a1 = y * (1 - core) + z * core
    a2 = z * (1 - core) + y * core
    stride1 = 2 * (1 - core) + 16 * core
    stride2 = 16 * (1 - core) + 2 * core
    base1 = d - a1 * stride1
    base2 = d - a2 * stride2
    partner = d + 1 - 2 * core

    def send(src, dst, t, kind, dom, hub):
        pltpu.make_async_remote_copy(
            src_ref=src, dst_ref=dst, send_sem=send_sem.at[t, kind], recv_sem=recv_sem.at[t, kind],
            device_id=(dom, hub), device_id_type=MESH,
        ).start()

    def wait_in(ref, t, kind):
        pltpu.make_async_copy(ref, ref, recv_sem.at[t, kind]).wait()

    def wait_out(ref, t, kind):
        pltpu.make_async_copy(ref, ref, send_sem.at[t, kind]).wait()

    def around(body, parts=(0, 1)):
        def both(dz, dy):
            chip = 16 * lax.rem(z + dz + 8, 8) + 2 * lax.rem(y + dy + 8, 8)
            body(chip + core)
            body(chip + 1 - core)

        def step(k, carry):
            kk = 14 - k + (14 - k) // 12
            a, b = kk // 4 + 1, lax.rem(kk, 4)
            both(a, b)
            both(-b, a)
            both(-a, -b)
            both(b, -a)
            return carry

        if 0 in parts:
            both(4, 4)
            both(4, 0)
            both(0, 4)
            lax.fori_loop(0, 7, step, 0)
        if 1 in parts:
            lax.fori_loop(7, 15, step, 0)
            body(partner)

    def peers_hub(body):
        for o in (1, 3, 2):
            body(lax.rem(j + o, 4), o - 1)

    loads = [
        pltpu.make_async_copy(src, dst, load_sem.at[i])
        for i, (src, dst) in enumerate((
            (tiles_hbm, tiles_ref), (index_hbm, index_ref), (cot_hbm, cot_ref),
            (hub_adj_hbm, hub_adj_ref), (hub_mask_hbm, hub_mask_ref), (tail_mask_hbm, tail_mask_ref),
        ))
    ]
    for load in loads:
        load.start()
    barrier = pltpu.get_barrier_semaphore()
    around(lambda p: pl.semaphore_signal(barrier, inc=1, device_id=(p, j), device_id_type=MESH))
    peers_hub(lambda h, o: pl.semaphore_signal(barrier, inc=1, device_id=(d, h), device_id_type=MESH))
    for load in loads:
        load.wait()
    pl.semaphore_wait(barrier, 130)

    cut = 32 // CUTS
    for i in range(CUTS):
        peers_hub(lambda h, o: send(
            tiles_ref.at[pl.ds(h * 32 + i * cut, cut)], tile_in.at[i, o], 0, TILE_RS + 2 * i, d, h))

    owner_row = jnp.broadcast_to(index_ref[1:2, :], (128, 128))
    block_row = jnp.broadcast_to(index_ref[2:3, :], (128, 128)).astype(F32)
    square = (128, 128)
    earlier = (owner_row == owner_row.astype(F32).T.astype(jnp.int32)) & (rows(square) < lanes(square))
    rank = jnp.sum(earlier.astype(F32), axis=0, keepdims=True)
    owned = owner_row == rows(square)
    pick0 = (owned & (rank < 0.5)).astype(F32)
    pick1 = (owned & (rank > 0.5)).astype(F32)
    block0 = jnp.sum(pick0 * block_row, axis=1, keepdims=True)
    block1 = jnp.sum(pick1 * block_row, axis=1, keepdims=True)
    def ways(p):
        c, py, pz = lax.rem(p, 2), lax.rem(p // 2, 8), p // 16
        return c, py * (1 - c) + pz * c, pz * (1 - c) + py * c

    second = 2 * ways(rows(square))[2]
    spot = jnp.where(lanes(square) == second, block0, 0.0) + jnp.where(lanes(square) == second + 1, block1, 0.0)
    at_core, at_one, _ = ways(lanes((16, 128)))
    gather = (8 * at_core + at_one == rows((16, 128))).astype(BF16)
    slot_index[...] = dot(gather, spot.astype(BF16)).reshape(2, 8, 1, 128)

    def go_one(sources, mid, t, kind):
        for o in AROUND:
            g, h = lax.rem(y + o, 8), lax.rem(z + o, 8)
            send(sources.at[0, g], mid.at[2 * y + core], t, kind, 16 * z + 2 * g, j)
            send(sources.at[1, h], mid.at[2 * z + core], t, kind, 16 * h + 2 * y + 1, j)
        send(sources.at[1 - core, a2], mid.at[2 * a2 + core], t, kind, partner, j)
        mid[2 * a1 + core] = sources[core, a1]

    def along_two(body):
        for o in AROUND:
            g = lax.rem(a2 + o, 8)
            body(g, base2 + g * stride2)

    go_one(slot_index, index_mid, 0, INDEX_ONE)

    adj = hub_adj_ref[...]
    adj_hi, adj_lo = split(adj)
    adj_t_hi, adj_t_lo = split(adj.T)

    def hub_start(t, grad):
        gh, gl = split(grad)
        hubp[t] = dot3(adj_t_hi, adj_t_lo, gh, gl)
        send(hubp.at[t, pl.ds((1 - core) * 256, 256)], pair_in.at[t], t, PAIR_RS, partner, j)

    def hub_one(t):
        wait_in(pair_in.at[t], t, PAIR_RS)
        one_out[t] = (hubp[t, pl.ds(core * 256, 256)] + pair_in[t]).reshape(8, 32, 256)
        for o in AROUND:
            g = lax.rem(a1 + o, 8)
            send(one_out.at[t, g], one_in.at[t, o - 1], t, ONE_RS, base1 + g * stride1, j)

    def hub_two(t):
        wait_in(one_in.at[t], t, ONE_RS)
        total = one_out[t, a1]
        for o in range(7):
            total = total + one_in[t, o]
        for b in range(4):
            for h in range(2):
                two_out[t, 2 * b + h] = total[8 * b:8 * b + 8, 128 * h:128 * h + 128]
        for o in AROUND:
            g = lax.rem(a2 + o, 8)
            send(two_out.at[t, g], two_in.at[t, o - 1], t, TWO_RS, base2 + g * stride2, j)

    def hub_back_two(t):
        wait_in(two_in.at[t], t, TWO_RS)
        total = two_out[t, a2]
        for o in range(7):
            total = total + two_in[t, o]
        first = pl.multiple_of(core * 256 + a1 * 32 + (a2 // 2) * 8, 8)
        left = pl.multiple_of(lax.rem(a2, 2) * 128, 128)
        mask = hub_mask_ref[t, pl.ds(first, 8), pl.ds(left, 128)].astype(F32)
        hub_full[t, core, a1, a2] = total * mask
        for o in AROUND:
            g = lax.rem(a2 + o, 8)
            send(hub_full.at[t, core, a1, a2], hub_full.at[t, core, a1, a2], t, TWO_AG, base2 + g * stride2, j)

    def hub_back_one(t):
        wait_in(two_in.at[t], t, TWO_AG)
        for o in AROUND:
            g = lax.rem(a1 + o, 8)
            send(hub_full.at[t, core, a1], hub_full.at[t, core, a1], t, ONE_AG, base1 + g * stride1, j)

    def hub_back_pair(t):
        wait_in(one_in.at[t], t, ONE_AG)
        send(hub_full.at[t, core], hub_full.at[t, core], t, PAIR_AG, partner, j)

    def hub_finish(t):
        wait_in(pair_in.at[t], t, PAIR_AG)
        full = hub_full[t].reshape(64, 2, 8, 128)
        item = jnp.concatenate([full[:, 0].reshape(512, 128), full[:, 1].reshape(512, 128)], axis=1)
        if t == 1:
            hub_out[...] = item
        ih, il = split(item)
        part = dot3(adj_hi, adj_lo, ih, il)
        low = lanes((64, 128)) < 64
        for h in range(4):
            half = part[:, 128 * (h // 2):128 * (h // 2) + 128]
            if h % 2 == 0:
                user_pack[t, h] = jnp.where(low, half[:64], roll64(half[64:]))
            else:
                user_pack[t, h] = jnp.where(low, roll64(half[:64]), half[64:])
        peers_hub(lambda h, o: send(user_pack.at[t, h], user_in.at[t, o], t, HUB_RS, d, h))

    left_half = pl.multiple_of((j // 2) * 128, 128)
    odd = lax.rem(j, 2)

    def mine(half):
        kept = jnp.where((lanes(half.shape) // 64) == odd, half, 0.0)
        return kept + roll64(kept)

    def halves(x):
        low = lanes(x.shape) < 64
        return jnp.concatenate([jnp.where(low, x, 0.0), jnp.where(low, 0.0, x)], axis=0)

    def tail_start(t, doubled, between):
        bh, bl = split(halves(doubled))
        both = side_by_side(bh, bl)
        for q in range(4):
            part = slice(256 * q, 256 * q + 256)
            x = fold(dot(tile_hi[part], both)) + dot(tile_lo[part], bh)
            tail_send[t, 32 * q:32 * q + 32] = x.reshape(32, 8, 128)
        tail_recv[t, d] = tail_send[t, d]
        around(lambda p: send(tail_send.at[t, p], tail_recv.at[t, d], t, TAIL_F, p, j), (0,))
        between()
        around(lambda p: send(tail_send.at[t, p], tail_recv.at[t, d], t, TAIL_F, p, j), (1,))

    def tail_turn(t, between):
        wait_in(tail_recv.at[t, pl.ds(0, 127)], t, TAIL_F)
        hi, lo = split(tail_recv[t].reshape(1024, 128))
        x = fold(dot(member[...], side_by_side(hi, lo)))
        low = lanes((256, 128)) < 64
        item = jnp.where(low, x[:256], x[256:])
        item = item + roll64(item)
        item = item * mine(tail_mask_ref[t, :, pl.ds(left_half, 128)].astype(F32))
        ih, il = split(halves(item))
        both = side_by_side(ih, il)
        for q in range(4):
            x = fold(dot(member_t[256 * q:256 * q + 256], both))
            reply_send[t, 32 * q:32 * q + 32] = x.reshape(32, 8, 128)
        reply_recv[t, d] = reply_send[t, d]
        around(lambda p: send(reply_send.at[t, p], reply_recv.at[t, d], t, TAIL_R, p, j), (0,))
        between()
        around(lambda p: send(reply_send.at[t, p], reply_recv.at[t, d], t, TAIL_R, p, j), (1,))
        if t == 1:
            tail_pack[j] = jnp.where(lanes((128, 128)) < 64, item[:128], item[128:])
            peers_hub(lambda h, o: send(tail_pack.at[j], tail_pack.at[j], 0, TAIL_OUT, d, h))

    def tail_end(t):
        wait_in(reply_recv.at[t, pl.ds(0, 127)], t, TAIL_R)
        rh, rl = split(reply_recv[t].reshape(1024, 128))
        x = fold(dot(tile_t_hi[...], side_by_side(rh, rl))) + dot(tile_t_lo[...], rh)
        low = lanes((64, 128)) < 64
        return jnp.where(low, x[:64] + roll64(x[128:192]), roll64(x[64:128]) + x[192:])

    def join(t, packed):
        wait_in(user_in.at[t], t, HUB_RS)
        packed = packed + user_pack[t, j] + user_in[t, 0] + user_in[t, 1] + user_in[t, 2]
        grad_pack[t, j] = packed
        peers_hub(lambda h, o: send(grad_pack.at[t, j], grad_pack.at[t, j], t, HUB_AG, d, h))
        low = lanes((64, 128)) < 64
        turned = roll64(packed)
        return jnp.concatenate([jnp.where(low, packed, turned), jnp.where(low, turned, packed)], axis=0)

    def unpack(t):
        wait_in(user_in.at[t], t, HUB_AG)
        low = lanes((64, 128)) < 64
        out = user_out if t == 1 else grad_ref
        for k in range(2):
            even, uneven = grad_pack[t, 2 * k], grad_pack[t, 2 * k + 1]
            out[:64, 128 * k:128 * k + 128] = jnp.where(low, even, roll64(uneven))
            out[64:, 128 * k:128 * k + 128] = jnp.where(low, roll64(even), uneven)

    hub_start(0, cot_ref[...])
    for i in range(CUTS):
        wait_in(tile_in.at[i], 0, TILE_RS + 2 * i)
        own = pl.ds(j * 32 + i * cut, cut)
        tile_sum[own] = tiles_ref[own] + tile_in[i, 0] + tile_in[i, 1] + tile_in[i, 2]
        peers_hub(lambda h, o: send(tile_sum.at[own], tile_sum.at[own], 0, TILE_AG + 2 * i, d, h))
    wait_in(index_mid.at[pl.ds(0, 15)], 0, INDEX_ONE)
    along_two(lambda g, p: send(index_mid, index_in.at[a2], 0, INDEX_TWO, p, j))
    index_in[a2] = index_mid[...]
    hub_one(0)
    hub_two(0)
    for i in range(CUTS):
        wait_in(tile_in.at[i], 0, TILE_AG + 2 * i)

    th, tl = split(tile_sum[...].reshape(128, 1024))
    both = jnp.concatenate([th, tl], axis=1)
    for s, pick in ((0, pick0), (1, pick1)):
        x = dot(pick.astype(BF16), both)
        placed = (x[:, :1024] + x[:, 1024:]).reshape(1024, 128)
        hi, lo = split(placed)
        tile_hi[:, 128 * s:128 * s + 128] = hi
        tile_lo[:, 128 * s:128 * s + 128] = lo
        hi, lo = split(placed.T)
        tile_t_hi[128 * s:128 * s + 128] = hi
        tile_t_lo[128 * s:128 * s + 128] = lo
    tail_start(0, mine(cot_ref[:, pl.ds(left_half, 128)]), lambda: hub_back_two(0))

    wait_in(index_in.at[pl.ds(0, 7)], 0, INDEX_TWO)
    shape = (1024, 128)
    sender = rows(shape) // 8
    turned = 16 * lax.rem(sender // 2, 8) + 2 * (sender // 16) + lax.rem(sender, 2)
    spread = (sender * (1 - core) + turned * core == lanes(shape)).astype(BF16)
    blocks = dot(spread, index_in[...].reshape(128, 128).astype(BF16))
    chosen = [jnp.sum(jnp.where(lanes(shape) == 2 * a2 + s, blocks, 0.0), axis=1, keepdims=True) for s in range(2)]
    place = jnp.where(lanes(shape) < 64, chosen[0], chosen[1]) * 8.0 + lax.rem(rows(shape), 8).astype(F32)
    place_t = place.T
    want_t = lanes((1024, 256)).astype(F32)
    want = rows((256, 1024)).astype(F32)
    for s in range(2):
        member_t[:, 256 * s:256 * s + 256] = (place[:, 64 * s:64 * s + 1] == want_t).astype(F32).astype(BF16)
        member[256 * s:256 * s + 256] = (place_t[64 * s:64 * s + 1] == want).astype(F32).astype(BF16)

    hub_back_one(0)
    tail_turn(0, lambda: hub_back_pair(0))
    hub_finish(0)

    def hub_again():
        unpack(0)
        hub_start(1, grad_ref[...])
        hub_one(1)

    tail_start(1, join(0, tail_end(0)), hub_again)
    hub_two(1)
    tail_turn(1, lambda: hub_back_two(1))
    hub_back_one(1)
    hub_back_pair(1)
    hub_finish(1)
    join(1, tail_end(1))
    unpack(1)

    wait_in(tail_pack.at[pl.ds(0, 3)], 0, TAIL_OUT)
    low = lanes((128, 128)) < 64
    for k in range(2):
        even, uneven = tail_pack[2 * k], tail_pack[2 * k + 1]
        tail_out[:128, 128 * k:128 * k + 128] = jnp.where(low, even, roll64(uneven))
        tail_out[128:, 128 * k:128 * k + 128] = jnp.where(low, roll64(even), uneven)

    for i in range(2 * CUTS):
        wait_out(tile_in.at[0], 0, TILE_RS + i)
    wait_out(index_mid.at[pl.ds(0, 15)], 0, INDEX_ONE)
    wait_out(index_in.at[pl.ds(0, 7)], 0, INDEX_TWO)
    wait_out(tail_pack.at[pl.ds(0, 3)], 0, TAIL_OUT)
    for t in range(2):
        wait_out(pair_in.at[t], t, PAIR_RS)
        wait_out(one_in.at[t], t, ONE_RS)
        wait_out(two_in.at[t], t, TWO_RS)
        wait_out(two_in.at[t], t, TWO_AG)
        wait_out(one_in.at[t], t, ONE_AG)
        wait_out(pair_in.at[t], t, PAIR_AG)
        wait_out(tail_recv.at[t, pl.ds(0, 127)], t, TAIL_F)
        wait_out(reply_recv.at[t, pl.ds(0, 127)], t, TAIL_R)
        wait_out(user_in.at[t], t, HUB_RS)
        wait_out(user_in.at[t], t, HUB_AG)


def local(user_cot, hub_adj, tiles, tile_index, hub_mask, tail_mask):
    vmem = pl.BlockSpec(memory_space=pltpu.VMEM)
    return pl.pallas_call(
        kernel,
        out_shape=(
            jax.ShapeDtypeStruct((128, 256), F32),
            jax.ShapeDtypeStruct((512, 256), F32),
            jax.ShapeDtypeStruct((256, 256), F32),
        ),
        in_specs=[pl.BlockSpec(memory_space=pltpu.HBM)] * 6,
        out_specs=(vmem,) * 3,
        scratch_shapes=[
            pltpu.VMEM((128, 256), F32),
            pltpu.VMEM((128, 512), F32),
            pltpu.VMEM((128, 8, 128), F32),
            pltpu.VMEM((3, 128), jnp.int32),
            pltpu.VMEM((2, 512, 256), jnp.int32),
            pltpu.VMEM((2, 256, 256), jnp.int32),
            pltpu.SemaphoreType.DMA((6,)),
            pltpu.VMEM((CUTS, 3, 32 // CUTS, 8, 128), F32),
            pltpu.VMEM((128, 8, 128), F32),
            pltpu.VMEM((2, 8, 1, 128), F32),
            pltpu.VMEM((16, 1, 128), F32),
            pltpu.VMEM((8, 16, 1, 128), F32),
            pltpu.VMEM((1024, 256), BF16),
            pltpu.VMEM((1024, 256), BF16),
            pltpu.VMEM((256, 1024), BF16),
            pltpu.VMEM((256, 1024), BF16),
            pltpu.VMEM((512, 1024), BF16),
            pltpu.VMEM((1024, 512), BF16),
            pltpu.VMEM((2, 512, 256), F32),
            pltpu.VMEM((2, 256, 256), F32),
            pltpu.VMEM((2, 8, 32, 256), F32),
            pltpu.VMEM((2, 7, 32, 256), F32),
            pltpu.VMEM((2, 8, 8, 128), F32),
            pltpu.VMEM((2, 7, 8, 128), F32),
            pltpu.VMEM((2, 2, 8, 8, 8, 128), F32),
            pltpu.VMEM((2, 128, 8, 128), F32),
            pltpu.VMEM((2, 128, 8, 128), F32),
            pltpu.VMEM((2, 128, 8, 128), F32),
            pltpu.VMEM((2, 128, 8, 128), F32),
            pltpu.VMEM((2, 4, 64, 128), F32),
            pltpu.VMEM((2, 3, 64, 128), F32),
            pltpu.VMEM((2, 4, 64, 128), F32),
            pltpu.VMEM((4, 128, 128), F32),
            pltpu.VMEM((128, 256), F32),
            pltpu.SemaphoreType.DMA((2, KINDS)),
            pltpu.SemaphoreType.DMA((2, KINDS)),
        ],
        compiler_params=pltpu.CompilerParams(
            collective_id=0, has_side_effects=True, vmem_limit_bytes=48 * 1024 * 1024
        ),
        cost_estimate=pl.CostEstimate(flops=4_000_000_000, bytes_accessed=4_000_000, transcendentals=0),
    )(user_cot, hub_adj, tiles, tile_index, hub_mask, tail_mask)


def solution(mesh):
    return jax.shard_map(
        local,
        mesh=mesh,
        in_specs=(
            P("dom", None),
            P("dom", "hub"),
            P(("dom", "hub"), None, None),
            P(None, ("dom", "hub")),
            P(None, "hub", None),
            P(None, "dom", None),
        ),
        out_specs=(P("dom", None), P("hub", None), P("dom", None)),
        check_vma=False,
    )
```

```python
import jax
import jax.numpy as jnp
from jax import lax
from jax.experimental import pallas as pl
from jax.experimental.pallas import tpu as pltpu
from jax.sharding import PartitionSpec as P

F32 = jnp.float32
BF16 = jnp.bfloat16
MESH = pl.DeviceIdType.MESH

(PAIR_RS, ONE_RS, TWO_RS, TWO_AG, ONE_AG, PAIR_AG, TAIL_F, TAIL_R,
 HUB_RS, HUB_AG, TAIL_OUT, INDEX_ONE, INDEX_TWO, TILE_RS, TILE_AG) = range(15)
CUTS = 4
KINDS = 14 + 2 * CUTS
AROUND = (4, 1, 7, 3, 5, 2, 6)


def split(x):
    hi = x.astype(BF16)
    return hi, (x - hi.astype(F32)).astype(BF16)


def dot(a, b, dims=((1,), (0,))):
    return lax.dot_general(a, b, (dims, ((), ())), preferred_element_type=F32)


def dot3(ah, al, bh, bl):
    return dot(ah, bh) + dot(ah, bl) + dot(al, bh)


def lanes(shape):
    return lax.broadcasted_iota(jnp.int32, shape, len(shape) - 1)


def rows(shape):
    return lax.broadcasted_iota(jnp.int32, shape, len(shape) - 2)


def roll64(x):
    return pltpu.roll(x, 64, 1)


def side_by_side(hi, lo):
    return jnp.concatenate([hi, lo], axis=1)


def fold(x):
    return x[:, :128] + x[:, 128:]


def kernel(
    cot_hbm, hub_adj_hbm, tiles_hbm, index_hbm, hub_mask_hbm, tail_mask_hbm,
    user_out, hub_out, tail_out,
    cot_ref, hub_adj_ref, tiles_ref, index_ref, hub_mask_ref, tail_mask_ref, load_sem,
    tile_in, tile_sum, slot_index, index_mid, index_in, tile_hi, tile_lo, tile_t_hi, tile_t_lo, member, member_t,
    hubp, pair_in, one_out, one_in, two_out, two_in, hub_full,
    tail_send, tail_recv, reply_send, reply_recv, user_pack, user_in, grad_pack, tail_pack, grad_ref,
    send_sem, recv_sem, ready_sem,
):
    d = lax.axis_index("dom")
    j = lax.axis_index("hub")
    core = lax.rem(d, 2)
    y = lax.rem(d // 2, 8)
    z = d // 16
    a1 = y * (1 - core) + z * core
    a2 = z * (1 - core) + y * core
    stride1 = 2 * (1 - core) + 16 * core
    stride2 = 16 * (1 - core) + 2 * core
    base1 = d - a1 * stride1
    base2 = d - a2 * stride2
    partner = d + 1 - 2 * core

    def send(src, dst, t, kind, dom, hub):
        pltpu.make_async_remote_copy(
            src_ref=src, dst_ref=dst, send_sem=send_sem.at[t, kind], recv_sem=recv_sem.at[t, kind],
            device_id=(dom, hub), device_id_type=MESH,
        ).start()

    def wait_in(ref, t, kind):
        pltpu.make_async_copy(ref, ref, recv_sem.at[t, kind]).wait()

    def wait_out(ref, t, kind):
        pltpu.make_async_copy(ref, ref, send_sem.at[t, kind]).wait()

    def around(body, parts=(0, 1)):
        def both(dz, dy):
            chip = 16 * lax.rem(z + dz + 8, 8) + 2 * lax.rem(y + dy + 8, 8)
            body(chip + core)
            body(chip + 1 - core)

        def step(k, carry):
            kk = 14 - k + (14 - k) // 12
            a, b = kk // 4 + 1, lax.rem(kk, 4)
            both(a, b)
            both(-b, a)
            both(-a, -b)
            both(b, -a)
            return carry

        if 0 in parts:
            both(4, 4)
            both(4, 0)
            both(0, 4)
            lax.fori_loop(0, 7, step, 0)
        if 1 in parts:
            lax.fori_loop(7, 15, step, 0)
            body(partner)

    def peers_hub(body):
        for o in (1, 3, 2):
            body(lax.rem(j + o, 4), o - 1)

    loads = [
        pltpu.make_async_copy(src, dst, load_sem.at[i])
        for i, (src, dst) in enumerate((
            (tiles_hbm, tiles_ref), (index_hbm, index_ref), (cot_hbm, cot_ref),
            (hub_adj_hbm, hub_adj_ref), (hub_mask_hbm, hub_mask_ref), (tail_mask_hbm, tail_mask_ref),
        ))
    ]
    for load in loads:
        load.start()
    barrier = pltpu.get_barrier_semaphore()
    for o in AROUND:
        g, h = lax.rem(y + o, 8), lax.rem(z + o, 8)
        for c in range(2):
            for p in (16 * z + 2 * g + c, 16 * h + 2 * y + c):
                pl.semaphore_signal(barrier, inc=1, device_id=(p, j), device_id_type=MESH)
    pl.semaphore_signal(barrier, inc=1, device_id=(partner, j), device_id_type=MESH)
    peers_hub(lambda h, o: pl.semaphore_signal(barrier, inc=1, device_id=(d, h), device_id_type=MESH))
    for load in loads:
        load.wait()
    pl.semaphore_wait(barrier, 32)

    cut = 32 // CUTS
    for i in range(CUTS):
        peers_hub(lambda h, o: send(
            tiles_ref.at[pl.ds(h * 32 + i * cut, cut)], tile_in.at[i, o], 0, TILE_RS + 2 * i, d, h))

    for o in AROUND:
        pl.semaphore_signal(
            ready_sem, inc=1, device_id=(16 * lax.rem(z + o, 8) + 2 * y + core, j), device_id_type=MESH
        )

    owner_row = jnp.broadcast_to(index_ref[1:2, :], (128, 128))
    block_row = jnp.broadcast_to(index_ref[2:3, :], (128, 128)).astype(F32)
    square = (128, 128)
    earlier = (owner_row == owner_row.astype(F32).T.astype(jnp.int32)) & (rows(square) < lanes(square))
    rank = jnp.sum(earlier.astype(F32), axis=0, keepdims=True)
    owned = owner_row == rows(square)
    pick0 = (owned & (rank < 0.5)).astype(F32)
    pick1 = (owned & (rank > 0.5)).astype(F32)
    block0 = jnp.sum(pick0 * block_row, axis=1, keepdims=True)
    block1 = jnp.sum(pick1 * block_row, axis=1, keepdims=True)
    def ways(p):
        c, py, pz = lax.rem(p, 2), lax.rem(p // 2, 8), p // 16
        return c, py * (1 - c) + pz * c, pz * (1 - c) + py * c

    second = 2 * ways(rows(square))[2]
    spot = jnp.where(lanes(square) == second, block0, 0.0) + jnp.where(lanes(square) == second + 1, block1, 0.0)
    at_core, at_one, _ = ways(lanes((16, 128)))
    gather = (8 * at_core + at_one == rows((16, 128))).astype(BF16)
    slot_index[...] = dot(gather, spot.astype(BF16)).reshape(2, 8, 1, 128)

    def go_one(sources, mid, t, kind):
        for o in AROUND:
            g, h = lax.rem(y + o, 8), lax.rem(z + o, 8)
            send(sources.at[0, g], mid.at[2 * y + core], t, kind, 16 * z + 2 * g, j)
            send(sources.at[1, h], mid.at[2 * z + core], t, kind, 16 * h + 2 * y + 1, j)
        send(sources.at[1 - core, a2], mid.at[2 * a2 + core], t, kind, partner, j)
        mid[2 * a1 + core] = sources[core, a1]

    def along_two(body):
        for o in AROUND:
            g = lax.rem(a2 + o, 8)
            body(g, base2 + g * stride2)

    go_one(slot_index, index_mid, 0, INDEX_ONE)

    adj = hub_adj_ref[...]
    adj_hi, adj_lo = split(adj)
    adj_t_hi, adj_t_lo = split(adj.T)

    def hub_start(t, grad):
        gh, gl = split(grad)
        hubp[t] = dot3(adj_t_hi, adj_t_lo, gh, gl)
        send(hubp.at[t, pl.ds((1 - core) * 256, 256)], pair_in.at[t], t, PAIR_RS, partner, j)

    def hub_one(t):
        wait_in(pair_in.at[t], t, PAIR_RS)
        one_out[t] = (hubp[t, pl.ds(core * 256, 256)] + pair_in[t]).reshape(8, 32, 256)
        for o in AROUND:
            g = lax.rem(a1 + o, 8)
            send(one_out.at[t, g], one_in.at[t, o - 1], t, ONE_RS, base1 + g * stride1, j)

    def hub_two(t):
        wait_in(one_in.at[t], t, ONE_RS)
        total = one_out[t, a1]
        for o in range(7):
            total = total + one_in[t, o]
        for b in range(4):
            for h in range(2):
                two_out[t, 2 * b + h] = total[8 * b:8 * b + 8, 128 * h:128 * h + 128]
        for o in AROUND:
            g = lax.rem(a2 + o, 8)
            send(two_out.at[t, g], two_in.at[t, o - 1], t, TWO_RS, base2 + g * stride2, j)

    def hub_back_two(t):
        wait_in(two_in.at[t], t, TWO_RS)
        total = two_out[t, a2]
        for o in range(7):
            total = total + two_in[t, o]
        first = pl.multiple_of(core * 256 + a1 * 32 + (a2 // 2) * 8, 8)
        left = pl.multiple_of(lax.rem(a2, 2) * 128, 128)
        mask = hub_mask_ref[t, pl.ds(first, 8), pl.ds(left, 128)].astype(F32)
        hub_full[t, core, a1, a2] = total * mask
        for o in AROUND:
            g = lax.rem(a2 + o, 8)
            send(hub_full.at[t, core, a1, a2], hub_full.at[t, core, a1, a2], t, TWO_AG, base2 + g * stride2, j)

    def hub_back_one(t):
        wait_in(two_in.at[t], t, TWO_AG)
        for o in AROUND:
            g = lax.rem(a1 + o, 8)
            send(hub_full.at[t, core, a1], hub_full.at[t, core, a1], t, ONE_AG, base1 + g * stride1, j)

    def hub_back_pair(t):
        wait_in(one_in.at[t], t, ONE_AG)
        send(hub_full.at[t, core], hub_full.at[t, core], t, PAIR_AG, partner, j)

    def hub_finish(t):
        wait_in(pair_in.at[t], t, PAIR_AG)
        full = hub_full[t].reshape(64, 2, 8, 128)
        item = jnp.concatenate([full[:, 0].reshape(512, 128), full[:, 1].reshape(512, 128)], axis=1)
        if t == 1:
            hub_out[...] = item
        ih, il = split(item)
        part = dot3(adj_hi, adj_lo, ih, il)
        low = lanes((64, 128)) < 64
        for h in range(4):
            half = part[:, 128 * (h // 2):128 * (h // 2) + 128]
            if h % 2 == 0:
                user_pack[t, h] = jnp.where(low, half[:64], roll64(half[64:]))
            else:
                user_pack[t, h] = jnp.where(low, roll64(half[:64]), half[64:])
        peers_hub(lambda h, o: send(user_pack.at[t, h], user_in.at[t, o], t, HUB_RS, d, h))

    left_half = pl.multiple_of((j // 2) * 128, 128)
    odd = lax.rem(j, 2)

    def mine(half):
        kept = jnp.where((lanes(half.shape) // 64) == odd, half, 0.0)
        return kept + roll64(kept)

    def halves(x):
        low = lanes(x.shape) < 64
        return jnp.concatenate([jnp.where(low, x, 0.0), jnp.where(low, 0.0, x)], axis=0)

    def tail_start(t, doubled, between):
        bh, bl = split(halves(doubled))
        both = side_by_side(bh, bl)
        for q in range(4):
            part = slice(256 * q, 256 * q + 256)
            x = fold(dot(tile_hi[part], both)) + dot(tile_lo[part], bh)
            tail_send[t, 32 * q:32 * q + 32] = x.reshape(32, 8, 128)
        tail_recv[t, d] = tail_send[t, d]
        around(lambda p: send(tail_send.at[t, p], tail_recv.at[t, d], t, TAIL_F, p, j), (0,))
        between()
        around(lambda p: send(tail_send.at[t, p], tail_recv.at[t, d], t, TAIL_F, p, j), (1,))

    def tail_turn(t, between):
        wait_in(tail_recv.at[t, pl.ds(0, 127)], t, TAIL_F)
        hi, lo = split(tail_recv[t].reshape(1024, 128))
        x = fold(dot(member[...], side_by_side(hi, lo)))
        low = lanes((256, 128)) < 64
        item = jnp.where(low, x[:256], x[256:])
        item = item + roll64(item)
        item = item * mine(tail_mask_ref[t, :, pl.ds(left_half, 128)].astype(F32))
        ih, il = split(halves(item))
        both = side_by_side(ih, il)
        for q in range(4):
            x = fold(dot(member_t[256 * q:256 * q + 256], both))
            reply_send[t, 32 * q:32 * q + 32] = x.reshape(32, 8, 128)
        reply_recv[t, d] = reply_send[t, d]
        around(lambda p: send(reply_send.at[t, p], reply_recv.at[t, d], t, TAIL_R, p, j), (0,))
        between()
        around(lambda p: send(reply_send.at[t, p], reply_recv.at[t, d], t, TAIL_R, p, j), (1,))
        if t == 1:
            tail_pack[j] = jnp.where(lanes((128, 128)) < 64, item[:128], item[128:])
            peers_hub(lambda h, o: send(tail_pack.at[j], tail_pack.at[j], 0, TAIL_OUT, d, h))

    def tail_end(t):
        wait_in(reply_recv.at[t, pl.ds(0, 127)], t, TAIL_R)
        rh, rl = split(reply_recv[t].reshape(1024, 128))
        x = fold(dot(tile_t_hi[...], side_by_side(rh, rl))) + dot(tile_t_lo[...], rh)
        low = lanes((64, 128)) < 64
        return jnp.where(low, x[:64] + roll64(x[128:192]), roll64(x[64:128]) + x[192:])

    def join(t, packed):
        wait_in(user_in.at[t], t, HUB_RS)
        packed = packed + user_pack[t, j] + user_in[t, 0] + user_in[t, 1] + user_in[t, 2]
        grad_pack[t, j] = packed
        peers_hub(lambda h, o: send(grad_pack.at[t, j], grad_pack.at[t, j], t, HUB_AG, d, h))
        low = lanes((64, 128)) < 64
        turned = roll64(packed)
        return jnp.concatenate([jnp.where(low, packed, turned), jnp.where(low, turned, packed)], axis=0)

    def unpack(t):
        wait_in(user_in.at[t], t, HUB_AG)
        low = lanes((64, 128)) < 64
        out = user_out if t == 1 else grad_ref
        for k in range(2):
            even, uneven = grad_pack[t, 2 * k], grad_pack[t, 2 * k + 1]
            out[:64, 128 * k:128 * k + 128] = jnp.where(low, even, roll64(uneven))
            out[64:, 128 * k:128 * k + 128] = jnp.where(low, roll64(even), uneven)

    hub_start(0, cot_ref[...])
    hub_one(0)
    for i in range(CUTS):
        wait_in(tile_in.at[i], 0, TILE_RS + 2 * i)
        own = pl.ds(j * 32 + i * cut, cut)
        tile_sum[own] = tiles_ref[own] + tile_in[i, 0] + tile_in[i, 1] + tile_in[i, 2]
        peers_hub(lambda h, o: send(tile_sum.at[own], tile_sum.at[own], 0, TILE_AG + 2 * i, d, h))
    wait_in(index_mid.at[pl.ds(0, 15)], 0, INDEX_ONE)
    along_two(lambda g, p: send(index_mid, index_in.at[a2], 0, INDEX_TWO, p, j))
    index_in[a2] = index_mid[...]
    hub_two(0)
    for i in range(CUTS):
        wait_in(tile_in.at[i], 0, TILE_AG + 2 * i)

    th, tl = split(tile_sum[...].reshape(128, 1024))
    both = jnp.concatenate([th, tl], axis=1)
    for s, pick in ((0, pick0), (1, pick1)):
        x = dot(pick.astype(BF16), both)
        placed = (x[:, :1024] + x[:, 1024:]).reshape(1024, 128)
        hi, lo = split(placed)
        tile_hi[:, 128 * s:128 * s + 128] = hi
        tile_lo[:, 128 * s:128 * s + 128] = lo
        hi, lo = split(placed.T)
        tile_t_hi[128 * s:128 * s + 128] = hi
        tile_t_lo[128 * s:128 * s + 128] = lo
    pl.semaphore_wait(ready_sem, 7)
    tail_start(0, mine(cot_ref[:, pl.ds(left_half, 128)]), lambda: hub_back_two(0))

    wait_in(index_in.at[pl.ds(0, 7)], 0, INDEX_TWO)
    shape = (1024, 128)
    sender = rows(shape) // 8
    turned = 16 * lax.rem(sender // 2, 8) + 2 * (sender // 16) + lax.rem(sender, 2)
    spread = (sender * (1 - core) + turned * core == lanes(shape)).astype(BF16)
    blocks = dot(spread, index_in[...].reshape(128, 128).astype(BF16))
    chosen = [jnp.sum(jnp.where(lanes(shape) == 2 * a2 + s, blocks, 0.0), axis=1, keepdims=True) for s in range(2)]
    place = jnp.where(lanes(shape) < 64, chosen[0], chosen[1]) * 8.0 + lax.rem(rows(shape), 8).astype(F32)
    place_t = place.T
    want_t = lanes((1024, 256)).astype(F32)
    want = rows((256, 1024)).astype(F32)
    for s in range(2):
        member_t[:, 256 * s:256 * s + 256] = (place[:, 64 * s:64 * s + 1] == want_t).astype(F32).astype(BF16)
        member[256 * s:256 * s + 256] = (place_t[64 * s:64 * s + 1] == want).astype(F32).astype(BF16)

    hub_back_one(0)
    tail_turn(0, lambda: hub_back_pair(0))
    hub_finish(0)

    def hub_again():
        unpack(0)
        hub_start(1, grad_ref[...])
        hub_one(1)

    tail_start(1, join(0, tail_end(0)), hub_again)
    hub_two(1)
    tail_turn(1, lambda: hub_back_two(1))
    hub_back_one(1)
    hub_back_pair(1)
    hub_finish(1)
    join(1, tail_end(1))
    unpack(1)

    wait_in(tail_pack.at[pl.ds(0, 3)], 0, TAIL_OUT)
    low = lanes((128, 128)) < 64
    for k in range(2):
        even, uneven = tail_pack[2 * k], tail_pack[2 * k + 1]
        tail_out[:128, 128 * k:128 * k + 128] = jnp.where(low, even, roll64(uneven))
        tail_out[128:, 128 * k:128 * k + 128] = jnp.where(low, roll64(even), uneven)

    for i in range(2 * CUTS):
        wait_out(tile_in.at[0], 0, TILE_RS + i)
    wait_out(index_mid.at[pl.ds(0, 15)], 0, INDEX_ONE)
    wait_out(index_in.at[pl.ds(0, 7)], 0, INDEX_TWO)
    wait_out(tail_pack.at[pl.ds(0, 3)], 0, TAIL_OUT)
    for t in range(2):
        wait_out(pair_in.at[t], t, PAIR_RS)
        wait_out(one_in.at[t], t, ONE_RS)
        wait_out(two_in.at[t], t, TWO_RS)
        wait_out(two_in.at[t], t, TWO_AG)
        wait_out(one_in.at[t], t, ONE_AG)
        wait_out(pair_in.at[t], t, PAIR_AG)
        wait_out(tail_recv.at[t, pl.ds(0, 127)], t, TAIL_F)
        wait_out(reply_recv.at[t, pl.ds(0, 127)], t, TAIL_R)
        wait_out(user_in.at[t], t, HUB_RS)
        wait_out(user_in.at[t], t, HUB_AG)


def local(user_cot, hub_adj, tiles, tile_index, hub_mask, tail_mask):
    vmem = pl.BlockSpec(memory_space=pltpu.VMEM)
    return pl.pallas_call(
        kernel,
        out_shape=(
            jax.ShapeDtypeStruct((128, 256), F32),
            jax.ShapeDtypeStruct((512, 256), F32),
            jax.ShapeDtypeStruct((256, 256), F32),
        ),
        in_specs=[pl.BlockSpec(memory_space=pltpu.HBM)] * 6,
        out_specs=(vmem,) * 3,
        scratch_shapes=[
            pltpu.VMEM((128, 256), F32),
            pltpu.VMEM((128, 512), F32),
            pltpu.VMEM((128, 8, 128), F32),
            pltpu.VMEM((3, 128), jnp.int32),
            pltpu.VMEM((2, 512, 256), jnp.int32),
            pltpu.VMEM((2, 256, 256), jnp.int32),
            pltpu.SemaphoreType.DMA((6,)),
            pltpu.VMEM((CUTS, 3, 32 // CUTS, 8, 128), F32),
            pltpu.VMEM((128, 8, 128), F32),
            pltpu.VMEM((2, 8, 1, 128), F32),
            pltpu.VMEM((16, 1, 128), F32),
            pltpu.VMEM((8, 16, 1, 128), F32),
            pltpu.VMEM((1024, 256), BF16),
            pltpu.VMEM((1024, 256), BF16),
            pltpu.VMEM((256, 1024), BF16),
            pltpu.VMEM((256, 1024), BF16),
            pltpu.VMEM((512, 1024), BF16),
            pltpu.VMEM((1024, 512), BF16),
            pltpu.VMEM((2, 512, 256), F32),
            pltpu.VMEM((2, 256, 256), F32),
            pltpu.VMEM((2, 8, 32, 256), F32),
            pltpu.VMEM((2, 7, 32, 256), F32),
            pltpu.VMEM((2, 8, 8, 128), F32),
            pltpu.VMEM((2, 7, 8, 128), F32),
            pltpu.VMEM((2, 2, 8, 8, 8, 128), F32),
            pltpu.VMEM((2, 128, 8, 128), F32),
            pltpu.VMEM((2, 128, 8, 128), F32),
            pltpu.VMEM((2, 128, 8, 128), F32),
            pltpu.VMEM((2, 128, 8, 128), F32),
            pltpu.VMEM((2, 4, 64, 128), F32),
            pltpu.VMEM((2, 3, 64, 128), F32),
            pltpu.VMEM((2, 4, 64, 128), F32),
            pltpu.VMEM((4, 128, 128), F32),
            pltpu.VMEM((128, 256), F32),
            pltpu.SemaphoreType.DMA((2, KINDS)),
            pltpu.SemaphoreType.DMA((2, KINDS)),
            pltpu.SemaphoreType.REGULAR,
        ],
        compiler_params=pltpu.CompilerParams(
            collective_id=0, has_side_effects=True, vmem_limit_bytes=48 * 1024 * 1024
        ),
        cost_estimate=pl.CostEstimate(flops=4_000_000_000, bytes_accessed=4_000_000, transcendentals=0),
    )(user_cot, hub_adj, tiles, tile_index, hub_mask, tail_mask)


def solution(mesh):
    return jax.shard_map(
        local,
        mesh=mesh,
        in_specs=(
            P("dom", None),
            P("dom", "hub"),
            P(("dom", "hub"), None, None),
            P(None, ("dom", "hub")),
            P(None, "hub", None),
            P(None, "dom", None),
        ),
        out_specs=(P("dom", None), P("hub", None), P("dom", None)),
        check_vma=False,
    )
```
